256 devices in a mesh: row: 8 (over y, core), col: 32 (over x, z).
Axes of the slice: x: 4, y: 4, z: 8, core: 2. Of those that a mesh axis runs over, the one named last changes fastest.
Arguments:
- matrix: float32 [4, 8, 1, 32, 512, 512], P(None, 'row', None, 'col'), may hold values from -1 to 5, as said below
Outputs:
- factored: float32 [4, 8, 1, 32, 512, 512], P(None, 'row', None, 'col')
The draws below stay inside these ranges and needn't reach their ends.
Inputs may be any that keep to these rules, and one draw needn't show every extreme that they name: `matrix`: symmetric and positive definite: a Matern kernel of site positions plus a symmetric perturbation plus a diagonal; only tiles with i >= j are read.
All inputs are finite; a program needn't handle non-finite values.
Results may differ from the reference program's by a relative error of at most 0.0001.
Values sent between devices are 32-bit elements; how exact they have to be, the bound alone decides.
No kernel may reach another device: no remote copies, remote signals or barrier semaphores. Data moves between devices by JAX's collectives and lax.ppermute only.
A program may use at most 128 MiB of HBM per device.

```python
import jax
import jax.numpy as jnp
from jax import lax

NB = 512
TC = 1
PANELS = 2
NT = 32
TR = 4
ORDER = 16384
N_ROW = 8
N_COL = 32


def draw_matrix(key, part):
    key = jax.random.fold_in(key, 11)
    key_x, key_y, key_noise = jax.random.split(key, 3)
    sites = jnp.arange(ORDER)
    xpos = ((sites // NB).astype(jnp.float32) + jax.random.uniform(key_x, (ORDER,), jnp.float32)) / NT
    ypos = ((sites % NB).astype(jnp.float32) + jax.random.uniform(key_y, (ORDER,), jnp.float32)) / NB
    reach = 0.15
    noise = jax.random.truncated_normal(key_noise, -4.0, 4.0, (ORDER, ORDER), jnp.float32)
    delta_x = xpos[:, None] - xpos[None, :]
    delta_y = ypos[:, None] - ypos[None, :]
    scaled = jnp.sqrt(delta_x * delta_x + delta_y * delta_y + 1e-12) * (1.7320508 / reach)
    kernel = (1.0 + scaled) * jnp.exp(-scaled)
    symmetric = (noise + noise.T) * (0.7 / jnp.sqrt(2.0 * ORDER))
    diagonal = jnp.where(sites[:, None] == sites[None, :], 2.5, 0.0)
    whole = (kernel + symmetric + diagonal).astype(jnp.float32)
    tiles = jnp.transpose(whole.reshape(NT, NB, NT, NB), (0, 2, 1, 3))
    return tiles.reshape(TR, N_ROW, TC, N_COL, NB, NB)


def setup_inputs(seed: int = 0) -> dict:
    seeds = jax.random.split(jax.random.key(seed), 2)
    return {
        "matrix": draw_matrix(jax.random.fold_in(seeds[1], 71), 0),
    }


def solve_panel(factor, panel):
    count = panel.shape[0]
    width = panel.shape[1]
    stacked = jnp.transpose(panel, (2, 0, 1)).reshape(width, count * width)
    solved = jax.scipy.linalg.solve_triangular(factor, stacked, lower=True)
    return jnp.transpose(solved.reshape(width, count, width), (1, 2, 0))

def reference(matrix):
    tiles = matrix.reshape(NT, NT, NB, NB)
    index = jnp.arange(NT)
    for panel_index in range(PANELS):
        factor = jnp.linalg.cholesky(tiles[panel_index, panel_index])
        solved = solve_panel(factor, tiles[:, panel_index])
        solved = jnp.where((index > panel_index)[:, None, None], solved, jnp.float32(0.0))

        def update(pair):
            row_tiles, left = pair
            return row_tiles - jnp.einsum('pq,jsq->jps', left, solved, precision=lax.Precision.HIGHEST)
        tiles = lax.map(update, (tiles, solved))
        new_column = jnp.where((index == panel_index)[:, None, None], factor[None], solved)
        keep_old = (index < panel_index)[:, None, None]
        tiles = tiles.at[:, panel_index].set(jnp.where(keep_old, tiles[:, panel_index], new_column))
    lower = index[:, None] >= index[None, :]
    tiles = jnp.where(lower[:, :, None, None], tiles, jnp.float32(0.0))
    return tiles.reshape(TR, N_ROW, TC, N_COL, NB, NB)
```

```python
import functools

import jax
import jax.numpy as jnp
from jax import lax
from jax.experimental import pallas as pl
from jax.experimental.pallas import tpu as pltpu
from jax.sharding import PartitionSpec as P

NZ = 8
HI = lax.Precision.HIGHEST
TN = ((1,), (1,))
NN = ((1,), (0,))
TT = ((0,), (0,))


def gid(r, c):
    return r * 32 + c


def permute(value, pairs):
    return lax.ppermute(value, ("row", "col"), pairs)


def dot(a, b, dims):
    return lax.dot_general(a, b, (dims, ((), ())), precision=HI, preferred_element_type=jnp.float32)


def factor128(a_ref, v_ref, u_ref):
    sub = lax.broadcasted_iota(jnp.int32, (8, 128), 0)
    lane = lax.broadcasted_iota(jnp.int32, (8, 128), 1)
    spread = lambda x: jnp.broadcast_to(x, (8, 128))
    for g in range(16):
        v_ref[8 * g : 8 * g + 8, :] = jnp.where(lane == sub + 8 * g, 1.0, 0.0).astype(jnp.float32)
    for g in range(16):
        rows = slice(8 * g, 8 * g + 8)
        ga = a_ref[rows, :]
        gv = v_ref[rows, :]
        c = [spread(ga[:, 8 * g + j : 8 * g + j + 1]) for j in range(8)]
        s = {(i, j): spread(c[j][i : i + 1, :]) for j in range(8) for i in range(j, 8)}
        inv = []
        l = {}
        for j in range(8):
            inv.append(lax.rsqrt(s[j, j]))
            for i in range(j + 1, 8):
                l[i, j] = s[i, j] * inv[j]
            for k in range(j + 1, 8):
                for i in range(k, 8):
                    s[i, k] = s[i, k] - l[i, j] * l[k, j]

        def solve(block):
            out = []
            for j in range(8):
                t = spread(block[j : j + 1, :])
                for k in range(j):
                    t = t - l[j, k] * out[k]
                out.append(t * inv[j])
            return out

        def back(r):
            q = [None] * 8
            for j in reversed(range(8)):
                t = r[j]
                for i in reversed(range(j + 1, 8)):
                    t = t - l[i, j] * q[i]
                q[j] = t * inv[j]
            return q

        def pack(r):
            t = r[0]
            for j in range(1, 8):
                t = jnp.where(sub == j, r[j], t)
            return t

        def tree(p):
            return ((p[0] + p[1]) + (p[2] + p[3])) + ((p[4] + p[5]) + (p[6] + p[7]))

        ra = solve(ga)
        rv = solve(gv)
        u_ref[rows, :] = jnp.where(lane >= sub + 8 * g, pack(ra), 0.0)
        v_ref[rows, :] = pack(rv)
        if g < 15:
            qa = back(ra)
            qv = back(rv)
            for h in range(g + 1, 16):
                below = slice(8 * h, 8 * h + 8)
                a = a_ref[below, :]
                v = v_ref[below, :]
                m = [spread(a[:, 8 * g + j : 8 * g + j + 1]) for j in range(8)]
                a_ref[below, :] = a - tree([m[j] * qa[j] for j in range(8)])
                v_ref[below, :] = v - tree([m[j] * qv[j] for j in range(8)])


def step_kernel(k, *refs):
    if k == 0:
        d_ref, w_ref, outs = refs[0], None, refs[1:]
    else:
        d_ref, w_ref, outs = refs[0], refs[1], refs[2:]
    if k < 7:
        p_ref, vrow_ref, dn_ref, wn_ref, a_ref, t_ref, u_ref = outs
    else:
        p_ref, vrow_ref, a_ref, t_ref, u_ref = outs
    a_ref[...] = d_ref[0:128, 0:128]
    factor128(a_ref, t_ref, u_ref)
    t = t_ref[...]
    p_ref[0:128, :] = u_ref[...].T
    if k:
        vrow_ref[:, 0 : 128 * k] = dot(t, w_ref[0:128, :], NN)
    vrow_ref[:, 128 * k :] = t
    if k < 7:
        p_ref[128:, :] = dot(d_ref[128:, 0:128], t, TN)
        for j in range(1, 8 - k):
            dn_ref[128 * (j - 1) :, 128 * (j - 1) : 128 * j] = d_ref[128 * j :, 128 * j : 128 * j + 128] - dot(
                p_ref[128 * j :, :], p_ref[128 * j : 128 * j + 128, :], TN
            )
        if k:
            wn_ref[:, 0 : 128 * k] = w_ref[128:, :] - dot(p_ref[128:, :], vrow_ref[:, 0 : 128 * k], NN)
        wn_ref[:, 128 * k :] = -dot(p_ref[128:, :], t, NN)


def step(k, d, w):
    n = (8 - k) * 128
    f = lambda *s: jax.ShapeDtypeStruct(s, jnp.float32)
    outs = [f(n, 128), f(128, 128 * (k + 1))]
    if k < 7:
        outs += [f(n - 128, n - 128), f(n - 128, 128 * (k + 1))]
    return pl.pallas_call(
        functools.partial(step_kernel, k),
        out_shape=outs,
        name=f"panel{k}",
        scratch_shapes=[pltpu.VMEM((128, 128), jnp.float32)] * 3,
        compiler_params=pltpu.CompilerParams(vmem_limit_bytes=40 * 2**20),
        cost_estimate=pl.CostEstimate(flops=8 * 10**9, bytes_accessed=8 * n * n, transcendentals=0),
    )(*((d,) if k == 0 else (d, w)))


def middle_kernel(c_ref, b_ref, *refs):
    ps, vs, m_ref, f_ref, y_ref = refs[0:8], refs[8:16], refs[16], refs[17], refs[18]
    c = c_ref[0]
    for k in range(8):
        y_ref[128 * k : 128 * k + 128, :] = dot(vs[k][...], b_ref[:, 0 : 128 * (k + 1)], TN)

    @pl.when(c < 2)
    def _():
        ri = lax.broadcasted_iota(jnp.int32, (1024, 512), 0)
        ci = lax.broadcasted_iota(jnp.int32, (1024, 512), 1)
        y_ref[...] = jnp.where(ri == ci + 512 * c, -1.0, 0.0).astype(jnp.float32)

    m_ref[...] = dot(vs[7][...], y_ref[896:1024, :], TT)
    for k in range(7):
        m_ref[0 : 128 * (k + 1), :] += dot(vs[k][...], y_ref[128 * k : 128 * k + 128, :], TT)

    f_ref[...] = jnp.zeros_like(f_ref)

    @pl.when(c == 0)
    def _():
        for k in range(4):
            f_ref[128 * k :, 128 * k : 128 * k + 128] = ps[k][0 : 512 - 128 * k, :]

    @pl.when(c != 0)
    def _():
        for k in range(4):
            f_ref[128 * k :, 128 * k : 128 * k + 128] = ps[k + 4][...]


def middle(my_col, b_col, ps, vs):
    vm = pl.BlockSpec(memory_space=pltpu.VMEM)
    return pl.pallas_call(
        middle_kernel,
        out_shape=[jax.ShapeDtypeStruct((1024, 512), jnp.float32), jax.ShapeDtypeStruct((512, 512), jnp.float32)],
        name="middle",
        in_specs=[pl.BlockSpec(memory_space=pltpu.SMEM)] + [vm] * 17,
        out_specs=[vm, vm],
        scratch_shapes=[pltpu.VMEM((1024, 512), jnp.float32)],
        compiler_params=pltpu.CompilerParams(vmem_limit_bytes=40 * 2**20),
        cost_estimate=pl.CostEstimate(flops=8 * 10**9, bytes_accessed=8 * 2**20, transcendentals=0),
    )(my_col.reshape(1), b_col, *ps, *vs)


def body(matrix):
    r = lax.axis_index("row")
    c = lax.axis_index("col")
    x, z = c // NZ, c % NZ
    local = matrix.reshape(4, 512, 512)
    R, Z = range(8), range(8)

    def spread_z(tile, xs):
        got = []
        for d in range(8):
            start = lax.rem(z + d, 8) * 64
            piece = lax.dynamic_slice_in_dim(tile, start, 64, 0)
            got.append(permute(piece, [(gid(a, 8 * b + p), gid(a, 8 * b + (p + d) % 8)) for a in R for b in xs for p in (0, 1)]))
        got = jnp.stack(got)
        q0 = lax.dynamic_index_in_dim(got, z, 0, keepdims=False)
        q1 = lax.dynamic_index_in_dim(got, lax.rem(z + 7, 8), 0, keepdims=False)
        return jnp.concatenate([q0, q1], axis=1)

    first = spread_z(local[0], [0])

    lead = jnp.where((x == 0) & (r < 2), first, 0.0)
    lead = lead + sum(permute(first, [(gid(k, b), gid(k, 8 * d + b)) for k in (0, 1) for b in Z]) for d in (1, 2, 3))
    lead = lead + sum(permute(lead, [(gid(k, b), gid(2 * d + k, b)) for k in (0, 1) for b in range(32)]) for d in (1, 2, 3))
    up = lambda v: permute(v, [(gid(a, 8 * b + e), gid(a, 8 * b + (e + 1) % 8)) for a in R for b in range(4) for e in Z])
    down = lambda v: permute(v, [(gid(a, 8 * b + e), gid(a, 8 * b + (e + 7) % 8)) for a in R for b in range(4) for e in Z])
    parts = [lead]
    left, right = lead, lead
    whole = jnp.zeros((8, 64, 1024), jnp.float32)
    whole = lax.dynamic_update_index_in_dim(whole, lead, z, 0)
    for s in range(1, 5):
        left = up(left)
        whole = lax.dynamic_update_index_in_dim(whole, left, lax.rem(z + 8 - s, 8), 0)
        if s < 4:
            right = down(right)
            whole = lax.dynamic_update_index_in_dim(whole, right, lax.rem(z + s, 8), 0)
    whole = whole.reshape(512, 1024)
    other = permute(whole, [(gid(a, b), gid(a ^ 1, b)) for a in R for b in range(32)])
    even = lax.rem(r, 2) == 0
    top = jnp.where(even, whole, other)
    bottom = jnp.where(even, other, whole)
    lead = jnp.concatenate([top, bottom], axis=0)

    slot = sum(permute(local[d], [(gid(a, p), gid(a, 8 * d + p)) for a in R for p in (0, 1)]) for d in (1, 2, 3))
    rest = spread_z(slot, [1, 2, 3])
    piece = jnp.where(x == 0, first, rest)
    rows = lax.all_gather(piece, "col", tiled=True)

    mine = permute(piece, [(gid(a, 8 * b + e), gid(e, 8 * b + a)) for a in R for b in range(4) for e in Z])
    got = jnp.zeros((8, 64, 1024), jnp.float32)
    quad = jnp.stack([mine] + [permute(mine, [(gid(a, b), gid((a + 2 * d) % 8, b)) for a in R for b in range(32)]) for d in (1, 2, 3)])
    pair = permute(quad, [(gid(a, b), gid(a ^ 1, b)) for a in R for b in range(32)])
    mate = r + 1 - 2 * lax.rem(r, 2)
    for d in range(4):
        got = lax.dynamic_update_index_in_dim(got, quad[d], lax.rem(r + 8 - 2 * d, 8), 0)
        got = lax.dynamic_update_index_in_dim(got, pair[d], lax.rem(mate + 8 - 2 * d, 8), 0)
    b_col = got.reshape(512, 1024)

    d, w, ps, vs = lead, None, [], []
    for k in range(8):
        o = step(k, d, w)
        ps.append(o[0])
        vs.append(o[1])
        if k < 7:
            d, w = o[2], o[3]
    m, factor = middle(c, b_col, ps, vs)

    product = lax.dot_general(rows, m, (NN, ((), ())), precision=lax.Precision.HIGH, preferred_element_type=jnp.float32)
    index = jnp.arange(4, dtype=jnp.int32)[:, None, None]
    out = jnp.where(c < 2, 0.0, local) - product.reshape(4, 512, 512)
    out = jnp.where((index == 0) & (c < 2) & (r == c), factor[None], out)
    out = jnp.where(8 * index + r >= c, out, 0.0)
    return out.reshape(4, 1, 1, 1, 512, 512)


def solution(mesh):
    placed = P(None, "row", None, "col", None, None)
    return jax.shard_map(body, mesh=mesh, in_specs=(placed,), out_specs=placed, check_vma=False)
```

```python
import functools

import jax
import jax.numpy as jnp
from jax import lax
from jax.experimental import pallas as pl
from jax.experimental.pallas import tpu as pltpu
from jax.sharding import PartitionSpec as P

NZ = 8
HI = lax.Precision.HIGHEST
TN = ((1,), (1,))
NN = ((1,), (0,))
TT = ((0,), (0,))


def gid(r, c):
    return r * 32 + c


def permute(value, pairs):
    return lax.ppermute(value, ("row", "col"), pairs)


def dot(a, b, dims):
    return lax.dot_general(a, b, (dims, ((), ())), precision=HI, preferred_element_type=jnp.float32)


def factor128(a_ref, v_ref, u_ref):
    sub = lax.broadcasted_iota(jnp.int32, (8, 128), 0)
    lane = lax.broadcasted_iota(jnp.int32, (8, 128), 1)
    spread = lambda x: jnp.broadcast_to(x, (8, 128))
    for g in range(16):
        v_ref[8 * g : 8 * g + 8, :] = jnp.where(lane == sub + 8 * g, 1.0, 0.0).astype(jnp.float32)
    for g in range(16):
        rows = slice(8 * g, 8 * g + 8)
        ga = a_ref[rows, :]
        gv = v_ref[rows, :]
        c = [spread(ga[:, 8 * g + j : 8 * g + j + 1]) for j in range(8)]
        s = {(i, j): spread(c[j][i : i + 1, :]) for j in range(8) for i in range(j, 8)}
        inv = []
        l = {}
        for j in range(8):
            inv.append(lax.rsqrt(s[j, j]))
            for i in range(j + 1, 8):
                l[i, j] = s[i, j] * inv[j]
            for k in range(j + 1, 8):
                for i in range(k, 8):
                    s[i, k] = s[i, k] - l[i, j] * l[k, j]

        def solve(block):
            out = []
            for j in range(8):
                t = spread(block[j : j + 1, :])
                for k in range(j):
                    t = t - l[j, k] * out[k]
                out.append(t * inv[j])
            return out

        def back(r):
            q = [None] * 8
            for j in reversed(range(8)):
                t = r[j]
                for i in reversed(range(j + 1, 8)):
                    t = t - l[i, j] * q[i]
                q[j] = t * inv[j]
            return q

        def pack(r):
            t = r[0]
            for j in range(1, 8):
                t = jnp.where(sub == j, r[j], t)
            return t

        def tree(p):
            return ((p[0] + p[1]) + (p[2] + p[3])) + ((p[4] + p[5]) + (p[6] + p[7]))

        ra = solve(ga)
        rv = solve(gv)
        u_ref[rows, :] = jnp.where(lane >= sub + 8 * g, pack(ra), 0.0)
        v_ref[rows, :] = pack(rv)
        if g < 15:
            qa = back(ra)
            qv = back(rv)
            for h in range(g + 1, 16):
                below = slice(8 * h, 8 * h + 8)
                a = a_ref[below, :]
                v = v_ref[below, :]
                m = [spread(a[:, 8 * g + j : 8 * g + j + 1]) for j in range(8)]
                a_ref[below, :] = a - tree([m[j] * qa[j] for j in range(8)])
                v_ref[below, :] = v - tree([m[j] * qv[j] for j in range(8)])


def step_kernel(k, *refs):
    if k == 0:
        d_ref, w_ref, outs = refs[0], None, refs[1:]
    else:
        d_ref, w_ref, outs = refs[0], refs[1], refs[2:]
    if k < 3:
        p_ref, vrow_ref, dn_ref, wn_ref, a_ref, t_ref, u_ref = outs
    else:
        p_ref, vrow_ref, a_ref, t_ref, u_ref = outs
    a_ref[...] = d_ref[0:128, 0:128]
    factor128(a_ref, t_ref, u_ref)
    t = t_ref[...]
    p_ref[0:128, :] = u_ref[...].T
    if k:
        vrow_ref[:, 0 : 128 * k] = dot(t, w_ref[0:128, :], NN)
    vrow_ref[:, 128 * k :] = t
    if k < 3:
        p_ref[128:, :] = dot(d_ref[128:, 0:128], t, TN)
        for j in range(1, 4 - k):
            dn_ref[128 * (j - 1) :, 128 * (j - 1) : 128 * j] = d_ref[128 * j :, 128 * j : 128 * j + 128] - dot(
                p_ref[128 * j :, :], p_ref[128 * j : 128 * j + 128, :], TN
            )
        if k:
            wn_ref[:, 0 : 128 * k] = w_ref[128:, :] - dot(p_ref[128:, :], vrow_ref[:, 0 : 128 * k], NN)
        wn_ref[:, 128 * k :] = -dot(p_ref[128:, :], t, NN)


def step(k, d, w):
    n = (4 - k) * 128
    f = lambda *s: jax.ShapeDtypeStruct(s, jnp.float32)
    outs = [f(n, 128), f(128, 128 * (k + 1))]
    if k < 3:
        outs += [f(n - 128, n - 128), f(n - 128, 128 * (k + 1))]
    return pl.pallas_call(
        functools.partial(step_kernel, k),
        out_shape=outs,
        name=f"panel{k}",
        scratch_shapes=[pltpu.VMEM((128, 128), jnp.float32)] * 3,
        compiler_params=pltpu.CompilerParams(vmem_limit_bytes=40 * 2**20),
        cost_estimate=pl.CostEstimate(flops=7 * 10**9, bytes_accessed=8 * n * n, transcendentals=0),
    )(*((d,) if k == 0 else (d, w)))


def whole_call(kernel, name, out_shape, scratch, flops, *args):
    vm = pl.BlockSpec(memory_space=pltpu.VMEM)
    sm = pl.BlockSpec(memory_space=pltpu.SMEM)
    return pl.pallas_call(
        kernel,
        out_shape=[jax.ShapeDtypeStruct(s, t) for s, t in out_shape],
        name=name,
        in_specs=[sm if a.dtype == jnp.int32 else vm for a in args],
        out_specs=[vm] * len(out_shape),
        scratch_shapes=[pltpu.VMEM(s, jnp.float32) for s in scratch],
        compiler_params=pltpu.CompilerParams(vmem_limit_bytes=48 * 2**20),
        cost_estimate=pl.CostEstimate(flops=flops, bytes_accessed=8 * 2**20, transcendentals=0),
    )(*args)


def factor512(d, between=lambda k, d: d):
    w, ps, vs = None, [], []
    for k in range(4):
        o = step(k, d, w)
        ps.append(o[0])
        vs.append(o[1])
        if k < 3:
            d, w = between(k, o[2]), o[3]
    return ps, vs


def unpack(pack_ref, v_s):
    v_s[...] = jnp.zeros_like(v_s)
    n = 0
    for k in range(4):
        for j in range(k + 1):
            v_s[128 * k : 128 * k + 128, 128 * j : 128 * j + 128] = pack_ref[128 * n : 128 * n + 128, :]
            n += 1


def pack(vs):
    return jnp.concatenate([vs[k][:, 128 * j : 128 * j + 128] for k in range(4) for j in range(k + 1)], axis=0)


def join_kernel(low_ref, next_ref, *refs):
    vs, pack_ref, d_ref, v_s, x_s = refs[0:4], *refs[4:8]
    v_s[...] = jnp.zeros_like(v_s)
    n = 0
    for k in range(4):
        v_s[128 * k : 128 * k + 128, 0 : 128 * (k + 1)] = vs[k][...]
        for j in range(k + 1):
            pack_ref[128 * n : 128 * n + 128, :] = vs[k][:, 128 * j : 128 * j + 128]
            n += 1
    x_s[...] = dot(low_ref[...], v_s[...], TN)
    d_ref[...] = next_ref[...] - dot(x_s[...], x_s[...], TN)
    q = dot(x_s[...], v_s[...], NN)
    for j in range(4):
        pack_ref[1280 + 512 * j : 1792 + 512 * j, :] = q[:, 128 * j : 128 * j + 128]


def unit(c, want):
    ri = lax.broadcasted_iota(jnp.int32, (512, 512), 0)
    ci = lax.broadcasted_iota(jnp.int32, (512, 512), 1)
    return jnp.where((ri == ci) & (c == want), -1.0, 0.0).astype(jnp.float32)


def early_kernel(c_ref, b_ref, pack_ref, r_ref, n_ref, b_s, v_s, q_s, y_s):
    c = c_ref[0]
    for i in range(4):
        b_s[128 * i : 128 * i + 128, :] = b_ref[(8 - i) % 8]
        q_s[:, 128 * i : 128 * i + 128] = pack_ref[1280 + 512 * i : 1792 + 512 * i, :]
    unpack(pack_ref, v_s)
    late = dot(b_s[...], q_s[...], TN)
    for i in range(4):
        r_ref[128 * i : 128 * i + 128, :] = b_ref[1 + i] - late[128 * i : 128 * i + 128, :]
    y_s[...] = dot(v_s[...], b_s[...], TN)

    @pl.when(c < 2)
    def _():
        y_s[...] = unit(c, 0)

    n_ref[...] = dot(v_s[...], y_s[...], TT)


def late_kernel(c_ref, pack0_ref, pack1_ref, r_ref, n_ref, hi_ref, lo_ref, v_s, q_s, y_s):
    c = c_ref[0]
    for i in range(4):
        q_s[:, 128 * i : 128 * i + 128] = pack0_ref[1280 + 512 * i : 1792 + 512 * i, :]
    unpack(pack1_ref, v_s)
    y_s[...] = dot(v_s[...], r_ref[...], TN)

    @pl.when(c < 2)
    def _():
        y_s[...] = unit(c, 1)

    m1 = dot(v_s[...], y_s[...], TT)
    y_s[...] = m1
    m0 = n_ref[...] - dot(q_s[...], y_s[...], TT)
    for i, m in enumerate((m0, m1)):
        hi = m.astype(jnp.bfloat16)
        hi_ref[512 * i : 512 * i + 512, :] = hi
        lo_ref[512 * i : 512 * i + 512, :] = (m - hi.astype(jnp.float32)).astype(jnp.bfloat16)


def update_kernel(place_ref, a_ref, r00_ref, r01_ref, r10_ref, r11_ref, hi_ref, lo_ref, f_ref, out_ref):
    r, c = place_ref[0], place_ref[1]
    slot, half = pl.program_id(0), pl.program_id(1)
    lower = 8 * slot + r >= c
    diagonal = (slot == 0) & (c < 2) & (r == c)

    @pl.when(lower & jnp.logical_not(diagonal))
    def _():
        total = jnp.where(c < 2, 0.0, a_ref[0])
        for p, refs in enumerate(((r00_ref, r01_ref), (r10_ref, r11_ref))):
            rows = jnp.concatenate([ref[0] for ref in refs], axis=0)
            hi = rows.astype(jnp.bfloat16)
            lo = (rows - hi.astype(jnp.float32)).astype(jnp.bfloat16)
            mh = hi_ref[512 * p : 512 * p + 512, :]
            ml = lo_ref[512 * p : 512 * p + 512, :]
            one = lambda u, v: lax.dot_general(u, v, (NN, ((), ())), preferred_element_type=jnp.float32)
            total = total - (one(hi, mh) + (one(hi, ml) + one(lo, mh)))
        out_ref[0] = total

    @pl.when(jnp.logical_not(lower))
    def _():
        out_ref[...] = jnp.zeros_like(out_ref)

    @pl.when(diagonal)
    def _():
        out_ref[0] = f_ref[pl.ds(pl.multiple_of(half * 256, 256), 256), :]


def update(place, local, rows, hi, lo, factor):
    vm = pl.BlockSpec(memory_space=pltpu.VMEM)
    tile = pl.BlockSpec((1, 256, 512), lambda s, h: (s, h, 0))
    part = lambda f: pl.BlockSpec((1, 128, 512), lambda s, h: (8 * s + f(h), 0, 0))
    return pl.pallas_call(
        update_kernel,
        grid=(4, 2),
        out_shape=jax.ShapeDtypeStruct((4, 512, 512), jnp.float32),
        name="update",
        in_specs=[
            pl.BlockSpec(memory_space=pltpu.SMEM),
            tile,
            part(lambda h: 6 * h),
            part(lambda h: 7 - 2 * h),
            part(lambda h: 1 + 2 * h),
            part(lambda h: 2 + 2 * h),
            vm,
            vm,
            vm,
        ],
        out_specs=tile,
        compiler_params=pltpu.CompilerParams(vmem_limit_bytes=60 * 2**20),
        cost_estimate=pl.CostEstimate(flops=6 * 10**9, bytes_accessed=16 * 2**20, transcendentals=0),
    )(place, local, rows, rows, rows, rows, hi, lo, factor)


def body(matrix):
    r = lax.axis_index("row")
    c = lax.axis_index("col")
    x, y, z = c // NZ, r // 2, c % NZ
    even = lax.rem(r, 2) == 0
    local = matrix.reshape(4, 512, 512)
    R, X, Z, C = range(8), range(4), range(8), range(32)
    tie = lax.optimization_barrier
    swap = lambda v: permute(v, [(gid(a, b), gid(a ^ 1, b)) for a in R for b in C])
    from_x0 = lambda v, d: permute(v, [(gid(a, p), gid(a, 8 * d + p)) for a in R for p in (0, 1)])
    over_y = lambda v, d: permute(v, [(gid(k, 0), gid(2 * d + k, 0)) for k in (0, 1)])
    over_z = lambda v, d: permute(v, [(gid(a, 0), gid(a, d)) for a in R])
    over_x = lambda v, d: permute(v, [(gid(a, b), gid(a, 8 * d + b)) for a in R for b in Z])
    shift_y = lambda v, d: permute(v, [(gid(a, b), gid((a + 2 * d) % 8, b)) for a in R for b in C])

    def stage_y(parts):
        return [jnp.where(y == 0, parts[0], 0.0)] + [over_y(parts[d], d) for d in (2, 1, 3)]

    def stage_z(got):
        return [jnp.where(z == 0, got, 0.0)] + [over_z(got, d) for d in (4, 3, 5, 2, 6, 1, 7)]

    def stage_x(got):
        return [jnp.where(x == 0, got, 0.0)] + [over_x(got, d) for d in (2, 1, 3)]

    def stage_ring(got):
        return [got] + [shift_y(got, d) for d in (1, 2, 3)]

    def gather_ring(parts):
        whole = jnp.zeros((4,) + parts[0].shape, jnp.float32)
        for d in range(4):
            whole = lax.dynamic_update_index_in_dim(whole, parts[d], lax.rem(y + 4 - d, 4), 0)
        return whole

    halves = lambda v: jnp.where(even, v[: v.shape[0] // 2], v[v.shape[0] // 2 :])
    quarters = lambda v: v.reshape(4, v.shape[0] // 4, 128)

    def both(mine):
        other = swap(mine)
        return jnp.concatenate([jnp.where(even, mine, other), jnp.where(even, other, mine)], axis=0)

    below = swap(local[0])
    corner = permute(local[0], [(gid(1, 1), gid(0, 0))])
    slots = [from_x0(local[1], 1), from_x0(local[3], 3)]
    piece = []
    for q in range(4):
        pairs = [(gid(a, p), gid(a, 16 + (1 + q if p else (8 - q) % 8))) for a in R for p in (0, 1)]
        piece.append(permute(local[2, 128 * q : 128 * q + 128], pairs))

    def between(k, d):
        nonlocal slots, piece
        if k == 2:
            slots, piece, d = tie((slots, piece, d))
            slot = jnp.where(x == 0, local[0], sum(slots))
            piece.append(jnp.where(z < 2, slot[0:128], 0.0))
            for e in (1, 2, 3):
                pairs = [(gid(a, 8 * b + p), gid(a, 8 * b + (1 + e if p else 8 - e))) for a in R for b in (0, 1, 3) for p in (0, 1)]
                piece.append(permute(slot[128 * e : 128 * e + 128], pairs))
        return d

    f32, b16 = jnp.float32, jnp.bfloat16
    tile, sq = (512, 512), ((512, 512), jnp.float32)
    me = c.reshape(1)
    full = lambda q: jnp.concatenate([jnp.pad(q[k], ((128 * k, 0), (0, 0))) for k in range(4)], axis=1)
    ps0, vs0 = factor512(local[0], between)
    pack0, corner = whole_call(join_kernel, "join", [((3328, 128), f32), sq], [tile, tile], 5 * 10**9, below, corner, *vs0)
    one = swap(pack0[1664:])
    one = [one, pack0[:1664]]
    mine, quad, rows = None, None, None

    def beside(k, d):
        nonlocal one, piece, mine, quad, rows
        if k == 0:
            one, piece, d = tie((one, piece, d))
            one = stage_y(quarters(jnp.where(even, one[1], one[0])))
            piece = sum(piece)
            rows = lax.all_gather(piece, "col", tiled=True).reshape(32, 128, 512)
            mine = permute(piece, [(gid(a, 8 * b + e), gid(e, 8 * b + a)) for a in R for b in X for e in Z])
        elif k == 1:
            one, mine, d = tie((one, mine, d))
            one = stage_z(sum(one))
            quad = stage_ring(mine)
        else:
            quad, d = tie((quad, d))
            quad.append(swap(jnp.stack(quad)))
        return d

    ps1, vs1 = factor512(corner, beside)
    factor1 = permute(full(ps1), [(gid(0, 0), gid(1, 1))])
    factor = jnp.where(c == 0, full(ps0), factor1)
    pack1 = pack(vs1)
    one, pack1 = tie((one, pack1))
    one = stage_x(sum(one))
    two = swap(pack1[640:])
    one, two = tie((one, two))
    one = stage_ring(sum(one))
    two = stage_y(quarters(jnp.where(even, pack1[:640], two)))
    one, two = tie((one, two))
    two = stage_z(sum(two))
    pack0 = both(gather_ring(one).reshape(1664, 128))
    two, pack0 = tie((two, pack0))
    two = stage_x(sum(two))
    mate = r + 1 - 2 * lax.rem(r, 2)
    b_col = jnp.zeros((8, 128, 512), jnp.float32)
    for d in range(4):
        b_col = lax.dynamic_update_index_in_dim(b_col, quad[d], lax.rem(r + 8 - 2 * d, 8), 0)
        b_col = lax.dynamic_update_index_in_dim(b_col, quad[4][d], lax.rem(mate + 8 - 2 * d, 8), 0)
    rest, first = whole_call(early_kernel, "early", [sq, sq], [tile] * 4, 6 * 10**9, me, b_col, pack0)
    two, rest = tie((two, rest))
    pack1 = both(gather_ring(stage_ring(sum(two))).reshape(640, 128))
    hi, lo = whole_call(late_kernel, "late", [((1024, 512), b16)] * 2, [tile] * 3, 6 * 10**9, me, pack0, pack1, rest, first)
    out = update(jnp.stack([r, c]), local, rows, hi, lo, factor)
    return out.reshape(4, 1, 1, 1, 512, 512)


def solution(mesh):
    placed = P(None, "row", None, "col", None, None)
    return jax.shard_map(body, mesh=mesh, in_specs=(placed,), out_specs=placed, check_vma=False)
```

```python
import functools

import jax
import jax.numpy as jnp
from jax import lax
from jax.experimental import pallas as pl
from jax.experimental.pallas import tpu as pltpu
from jax.sharding import PartitionSpec as P

NZ = 8
HI = lax.Precision.HIGHEST
TN = ((1,), (1,))
NN = ((1,), (0,))
TT = ((0,), (0,))


def gid(r, c):
    return r * 32 + c


def permute(value, pairs):
    return lax.ppermute(value, ("row", "col"), pairs)


def dot(a, b, dims):
    return lax.dot_general(a, b, (dims, ((), ())), precision=HI, preferred_element_type=jnp.float32)


def factor128(a_ref, v_ref, u_ref):
    sub = lax.broadcasted_iota(jnp.int32, (8, 128), 0)
    lane = lax.broadcasted_iota(jnp.int32, (8, 128), 1)
    spread = lambda x: jnp.broadcast_to(x, (8, 128))
    for g in range(16):
        v_ref[8 * g : 8 * g + 8, :] = jnp.where(lane == sub + 8 * g, 1.0, 0.0).astype(jnp.float32)
    for g in range(16):
        rows = slice(8 * g, 8 * g + 8)
        ga = a_ref[rows, :]
        gv = v_ref[rows, :]
        c = [spread(ga[:, 8 * g + j : 8 * g + j + 1]) for j in range(8)]
        s = {(i, j): spread(c[j][i : i + 1, :]) for j in range(8) for i in range(j, 8)}
        inv = []
        l = {}
        for j in range(8):
            inv.append(lax.rsqrt(s[j, j]))
            for i in range(j + 1, 8):
                l[i, j] = s[i, j] * inv[j]
            for k in range(j + 1, 8):
                for i in range(k, 8):
                    s[i, k] = s[i, k] - l[i, j] * l[k, j]

        def solve(block):
            out = []
            for j in range(8):
                t = spread(block[j : j + 1, :])
                for k in range(j):
                    t = t - l[j, k] * out[k]
                out.append(t * inv[j])
            return out

        def back(r):
            q = [None] * 8
            for j in reversed(range(8)):
                t = r[j]
                for i in reversed(range(j + 1, 8)):
                    t = t - l[i, j] * q[i]
                q[j] = t * inv[j]
            return q

        def pack(r):
            t = r[0]
            for j in range(1, 8):
                t = jnp.where(sub == j, r[j], t)
            return t

        def tree(p):
            return ((p[0] + p[1]) + (p[2] + p[3])) + ((p[4] + p[5]) + (p[6] + p[7]))

        ra = solve(ga)
        rv = solve(gv)
        u_ref[rows, :] = jnp.where(lane >= sub + 8 * g, pack(ra), 0.0)
        v_ref[rows, :] = pack(rv)
        if g < 15:
            qa = back(ra)
            qv = back(rv)
            for h in range(g + 1, 16):
                below = slice(8 * h, 8 * h + 8)
                a = a_ref[below, :]
                v = v_ref[below, :]
                m = [spread(a[:, 8 * g + j : 8 * g + j + 1]) for j in range(8)]
                a_ref[below, :] = a - tree([m[j] * qa[j] for j in range(8)])
                v_ref[below, :] = v - tree([m[j] * qv[j] for j in range(8)])


def step_kernel(k, *refs):
    if k == 0:
        d_ref, w_ref, outs = refs[0], None, refs[1:]
    else:
        d_ref, w_ref, outs = refs[0], refs[1], refs[2:]
    if k < 3:
        p_ref, vrow_ref, dn_ref, wn_ref, a_ref, t_ref, u_ref = outs
    else:
        p_ref, vrow_ref, a_ref, t_ref, u_ref = outs
    a_ref[...] = d_ref[0:128, 0:128]
    factor128(a_ref, t_ref, u_ref)
    t = t_ref[...]
    p_ref[0:128, :] = u_ref[...].T
    if k:
        vrow_ref[:, 0 : 128 * k] = dot(t, w_ref[0:128, :], NN)
    vrow_ref[:, 128 * k :] = t
    if k < 3:
        p_ref[128:, :] = dot(d_ref[128:, 0:128], t, TN)
        for j in range(1, 4 - k):
            dn_ref[128 * (j - 1) :, 128 * (j - 1) : 128 * j] = d_ref[128 * j :, 128 * j : 128 * j + 128] - dot(
                p_ref[128 * j :, :], p_ref[128 * j : 128 * j + 128, :], TN
            )
        if k:
            wn_ref[:, 0 : 128 * k] = w_ref[128:, :] - dot(p_ref[128:, :], vrow_ref[:, 0 : 128 * k], NN)
        wn_ref[:, 128 * k :] = -dot(p_ref[128:, :], t, NN)


def step(k, d, w):
    n = (4 - k) * 128
    f = lambda *s: jax.ShapeDtypeStruct(s, jnp.float32)
    outs = [f(n, 128), f(128, 128 * (k + 1))]
    if k < 3:
        outs += [f(n - 128, n - 128), f(n - 128, 128 * (k + 1))]
    return pl.pallas_call(
        functools.partial(step_kernel, k),
        out_shape=outs,
        name=f"panel{k}",
        scratch_shapes=[pltpu.VMEM((128, 128), jnp.float32)] * 3,
        compiler_params=pltpu.CompilerParams(vmem_limit_bytes=40 * 2**20),
        cost_estimate=pl.CostEstimate(flops=7 * 10**9, bytes_accessed=8 * n * n, transcendentals=0),
    )(*((d,) if k == 0 else (d, w)))


def whole_call(kernel, name, out_shape, scratch, flops, *args):
    vm = pl.BlockSpec(memory_space=pltpu.VMEM)
    sm = pl.BlockSpec(memory_space=pltpu.SMEM)
    return pl.pallas_call(
        kernel,
        out_shape=[jax.ShapeDtypeStruct(s, t) for s, t in out_shape],
        name=name,
        in_specs=[sm if a.dtype == jnp.int32 else vm for a in args],
        out_specs=[vm] * len(out_shape),
        scratch_shapes=[pltpu.VMEM(s, jnp.float32) for s in scratch],
        compiler_params=pltpu.CompilerParams(vmem_limit_bytes=48 * 2**20),
        cost_estimate=pl.CostEstimate(flops=flops, bytes_accessed=8 * 2**20, transcendentals=0),
    )(*args)


def factor512(d, between=lambda k, d: d):
    w, ps, vs = None, [], []
    for k in range(4):
        o = step(k, d, w)
        ps.append(o[0])
        vs.append(o[1])
        if k < 3:
            d, w = between(k, o[2]), o[3]
    return ps, vs


def unpack(pack_ref, v_s):
    v_s[...] = jnp.zeros_like(v_s)
    n = 0
    for k in range(4):
        for j in range(k + 1):
            v_s[128 * k : 128 * k + 128, 128 * j : 128 * j + 128] = pack_ref[128 * n : 128 * n + 128, :]
            n += 1


def pack(vs):
    return jnp.concatenate([vs[k][:, 128 * j : 128 * j + 128] for k in range(4) for j in range(k + 1)], axis=0)


def join_kernel(low_ref, next_ref, *refs):
    vs, pack_ref, d_ref, v_s, x_s = refs[0:4], *refs[4:8]
    v_s[...] = jnp.zeros_like(v_s)
    n = 0
    for k in range(4):
        v_s[128 * k : 128 * k + 128, 0 : 128 * (k + 1)] = vs[k][...]
        for j in range(k + 1):
            pack_ref[128 * n : 128 * n + 128, :] = vs[k][:, 128 * j : 128 * j + 128]
            n += 1
    x_s[...] = dot(low_ref[...], v_s[...], TN)
    d_ref[...] = next_ref[...] - dot(x_s[...], x_s[...], TN)
    q = dot(x_s[...], v_s[...], NN)
    for j in range(4):
        pack_ref[1280 + 512 * j : 1792 + 512 * j, :] = q[:, 128 * j : 128 * j + 128]


def unit(c, want):
    ri = lax.broadcasted_iota(jnp.int32, (512, 512), 0)
    ci = lax.broadcasted_iota(jnp.int32, (512, 512), 1)
    return jnp.where((ri == ci) & (c == want), -1.0, 0.0).astype(jnp.float32)


def early_kernel(c_ref, b_ref, pack_ref, r_ref, n_ref, b_s, v_s, q_s, y_s):
    c = c_ref[0]
    for i in range(4):
        b_s[128 * i : 128 * i + 128, :] = b_ref[(8 - i) % 8]
        q_s[:, 128 * i : 128 * i + 128] = pack_ref[1280 + 512 * i : 1792 + 512 * i, :]
    unpack(pack_ref, v_s)
    late = dot(b_s[...], q_s[...], TN)
    for i in range(4):
        r_ref[128 * i : 128 * i + 128, :] = b_ref[1 + i] - late[128 * i : 128 * i + 128, :]
    y_s[...] = dot(v_s[...], b_s[...], TN)

    @pl.when(c < 2)
    def _():
        y_s[...] = unit(c, 0)

    n_ref[...] = dot(v_s[...], y_s[...], TT)


def late_kernel(c_ref, pack0_ref, pack1_ref, r_ref, n_ref, hi_ref, lo_ref, v_s, q_s, y_s):
    c = c_ref[0]
    for i in range(4):
        q_s[:, 128 * i : 128 * i + 128] = pack0_ref[1280 + 512 * i : 1792 + 512 * i, :]
    unpack(pack1_ref, v_s)
    y_s[...] = dot(v_s[...], r_ref[...], TN)

    @pl.when(c < 2)
    def _():
        y_s[...] = unit(c, 1)

    m1 = dot(v_s[...], y_s[...], TT)
    y_s[...] = m1
    m0 = n_ref[...] - dot(q_s[...], y_s[...], TT)
    for i, m in enumerate((m0, m1)):
        hi = m.astype(jnp.bfloat16)
        hi_ref[512 * i : 512 * i + 512, :] = hi
        lo_ref[512 * i : 512 * i + 512, :] = (m - hi.astype(jnp.float32)).astype(jnp.bfloat16)


def update_kernel(place_ref, a_ref, *refs):
    hi_ref, lo_ref, f_ref, out_ref = refs[8:]
    r, c = place_ref[0], place_ref[1]
    slot = pl.program_id(0)
    lower = 8 * slot + r >= c
    diagonal = (slot == 0) & (c < 2) & (r == c)

    @pl.when(lower & jnp.logical_not(diagonal))
    def _():
        total = jnp.where(c < 2, 0.0, a_ref[0])
        for p in range(2):
            rows = jnp.concatenate([ref[0] for ref in refs[4 * p : 4 * p + 4]], axis=0)
            hi = rows.astype(jnp.bfloat16)
            lo = (rows - hi.astype(jnp.float32)).astype(jnp.bfloat16)
            mh = hi_ref[512 * p : 512 * p + 512, :]
            ml = lo_ref[512 * p : 512 * p + 512, :]
            one = lambda u, v: lax.dot_general(u, v, (NN, ((), ())), preferred_element_type=jnp.float32)
            total = total - (one(hi, mh) + (one(hi, ml) + one(lo, mh)))
        out_ref[0] = total

    @pl.when(jnp.logical_not(lower))
    def _():
        out_ref[...] = jnp.zeros_like(out_ref)

    @pl.when(diagonal)
    def _():
        out_ref[0] = f_ref[...]


def update(place, local, rows, hi, lo, factor):
    vm = pl.BlockSpec(memory_space=pltpu.VMEM)
    tile = pl.BlockSpec((1, 512, 512), lambda s: (s, 0, 0))
    part = lambda q: pl.BlockSpec((1, 128, 512), lambda s: (8 * s + q, 0, 0))
    return pl.pallas_call(
        update_kernel,
        grid=(4,),
        out_shape=jax.ShapeDtypeStruct((4, 512, 512), jnp.float32),
        name="update",
        in_specs=[pl.BlockSpec(memory_space=pltpu.SMEM), tile] + [part(q) for q in (0, 7, 6, 5, 1, 2, 3, 4)] + [vm] * 3,
        out_specs=tile,
        compiler_params=pltpu.CompilerParams(vmem_limit_bytes=60 * 2**20),
        cost_estimate=pl.CostEstimate(flops=6 * 10**9, bytes_accessed=16 * 2**20, transcendentals=0),
    )(place, local, *[rows] * 8, hi, lo, factor)


def body(matrix):
    r = lax.axis_index("row")
    c = lax.axis_index("col")
    x, y, z = c // NZ, r // 2, c % NZ
    even = lax.rem(r, 2) == 0
    local = matrix.reshape(4, 512, 512)
    R, X, Z, C = range(8), range(4), range(8), range(32)
    tie = lax.optimization_barrier
    swap = lambda v: permute(v, [(gid(a, b), gid(a ^ 1, b)) for a in R for b in C])
    from_x0 = lambda v, d: permute(v, [(gid(a, p), gid(a, 8 * d + p)) for a in R for p in (0, 1)])
    over_y = lambda v, d: permute(v, [(gid(k, 0), gid(2 * d + k, 0)) for k in (0, 1)])
    over_z = lambda v, d: permute(v, [(gid(a, 0), gid(a, d)) for a in R])
    over_x = lambda v, d: permute(v, [(gid(a, b), gid(a, 8 * d + b)) for a in R for b in Z])
    shift_y = lambda v, d: permute(v, [(gid(a, b), gid((a + 2 * d) % 8, b)) for a in R for b in C])

    def stage_y(parts):
        return [jnp.where(y == 0, parts[0], 0.0)] + [over_y(parts[d], d) for d in (2, 1, 3)]

    def stage_z(got):
        return [jnp.where(z == 0, got, 0.0)] + [over_z(got, d) for d in (4, 3, 5, 2, 6, 1, 7)]

    def stage_x(got):
        return [jnp.where(x == 0, got, 0.0)] + [over_x(got, d) for d in (2, 1, 3)]

    def stage_ring(got):
        return [got] + [shift_y(got, d) for d in (1, 2, 3)]

    def gather_ring(parts):
        whole = jnp.zeros((4,) + parts[0].shape, jnp.float32)
        for d in range(4):
            whole = lax.dynamic_update_index_in_dim(whole, parts[d], lax.rem(y + 4 - d, 4), 0)
        return whole

    halves = lambda v: jnp.where(even, v[: v.shape[0] // 2], v[v.shape[0] // 2 :])
    quarters = lambda v: v.reshape(4, v.shape[0] // 4, 128)

    slots = [from_x0(local[1], 1), from_x0(local[3], 3), from_x0(local[2], 2)]
    piece, below, corner = [], None, None

    def between(k, d):
        nonlocal below, corner
        if k == 0:
            held, d = tie((local, d))
            below = swap(held[0])
            corner = permute(held[0], [(gid(1, 1), gid(0, 0))])
        return d

    f32, b16 = jnp.float32, jnp.bfloat16
    tile, sq = (512, 512), ((512, 512), jnp.float32)
    me = c.reshape(1)
    full = lambda q: jnp.concatenate([jnp.pad(q[k], ((128 * k, 0), (0, 0))) for k in range(4)], axis=1)
    ps0, vs0 = factor512(local[0], between)
    pack0, corner = whole_call(join_kernel, "join", [((3328, 128), f32), sq], [tile, tile], 5 * 10**9, below, corner, *vs0)
    one = swap(pack0[1664:])
    rows = None

    def beside(k, d):
        nonlocal one, slots, piece, rows
        if k == 0:
            one, slots, d = tie((one, slots, d))
            one = stage_y(quarters(jnp.where(even, pack0[:1664], one)))
            slot = jnp.where(x == 0, local[0], sum(slots))
            piece.append(jnp.where(z < 2, slot[0:128], 0.0))
            for e in (1, 2, 3):
                pairs = [(gid(a, 8 * b + p), gid(a, 8 * b + (1 + e if p else 8 - e))) for a in R for b in X for p in (0, 1)]
                piece.append(permute(slot[128 * e : 128 * e + 128], pairs))
        elif k == 1:
            one, d = tie((one, d))
            one = stage_z(sum(one))
        else:
            piece, d = tie((piece, d))
            piece = sum(piece)
            rows = lax.all_gather(piece, "col", tiled=True).reshape(32, 128, 512)
        return d

    def both(mine):
        other = swap(mine)
        return jnp.concatenate([jnp.where(even, mine, other), jnp.where(even, other, mine)], axis=0)

    ps1, vs1 = factor512(corner, beside)
    pack1 = pack(vs1)
    two, one, piece = tie((swap(pack1[640:]), one, piece))
    mine = permute(piece, [(gid(a, 8 * b + e), gid(e, 8 * b + a)) for a in R for b in X for e in Z])
    one = stage_x(sum(one))
    two = stage_y(quarters(jnp.where(even, pack1[:640], two)))
    one, two, ps1, mine = tie((one, two, ps1, mine))
    one, two, quad = stage_ring(sum(one)), stage_z(sum(two)), stage_ring(mine)
    factor1 = permute(full(ps1), [(gid(0, 0), gid(1, 1))])
    factor = jnp.where(c == 0, full(ps0), factor1)
    one, two, quad = tie((one, two, quad))
    pack0 = both(gather_ring(one).reshape(1664, 128))
    quad.append(swap(jnp.stack(quad)))
    two = stage_x(sum(two))
    two, quad, pack0 = tie((two, quad, pack0))
    two = stage_ring(sum(two))
    mate = r + 1 - 2 * lax.rem(r, 2)
    b_col = jnp.zeros((8, 128, 512), jnp.float32)
    for d in range(4):
        b_col = lax.dynamic_update_index_in_dim(b_col, quad[d], lax.rem(r + 8 - 2 * d, 8), 0)
        b_col = lax.dynamic_update_index_in_dim(b_col, quad[4][d], lax.rem(mate + 8 - 2 * d, 8), 0)
    rest, first = whole_call(early_kernel, "early", [sq, sq], [tile] * 4, 6 * 10**9, me, b_col, pack0)
    two, rest = tie((two, rest))
    pack1 = both(gather_ring(two).reshape(640, 128))
    hi, lo = whole_call(late_kernel, "late", [((1024, 512), b16)] * 2, [tile] * 3, 6 * 10**9, me, pack0, pack1, rest, first)
    out = update(jnp.stack([r, c]), local, rows, hi, lo, factor)
    return out.reshape(4, 1, 1, 1, 512, 512)


def solution(mesh):
    placed = P(None, "row", None, "col", None, None)
    return jax.shard_map(body, mesh=mesh, in_specs=(placed,), out_specs=placed, check_vma=False)
```

```python
import functools

import jax
import jax.numpy as jnp
from jax import lax
from jax.experimental import pallas as pl
from jax.experimental.pallas import tpu as pltpu
from jax.sharding import PartitionSpec as P

NZ = 8
HI = lax.Precision.HIGHEST
TN = ((1,), (1,))
NN = ((1,), (0,))
TT = ((0,), (0,))


def gid(r, c):
    return r * 32 + c


def permute(value, pairs):
    return lax.ppermute(value, ("row", "col"), pairs)


def dot(a, b, dims):
    return lax.dot_general(a, b, (dims, ((), ())), precision=HI, preferred_element_type=jnp.float32)


def factor128(a_ref, v_ref, u_ref):
    sub = lax.broadcasted_iota(jnp.int32, (8, 128), 0)
    lane = lax.broadcasted_iota(jnp.int32, (8, 128), 1)
    spread = lambda x: jnp.broadcast_to(x, (8, 128))
    for g in range(16):
        v_ref[8 * g : 8 * g + 8, :] = jnp.where(lane == sub + 8 * g, 1.0, 0.0).astype(jnp.float32)
    for g in range(16):
        rows = slice(8 * g, 8 * g + 8)
        ga = a_ref[rows, :]
        gv = v_ref[rows, :]
        c = [spread(ga[:, 8 * g + j : 8 * g + j + 1]) for j in range(8)]
        s = {(i, j): spread(c[j][i : i + 1, :]) for j in range(8) for i in range(j, 8)}
        inv = []
        l = {}
        for j in range(8):
            inv.append(lax.rsqrt(s[j, j]))
            for i in range(j + 1, 8):
                l[i, j] = s[i, j] * inv[j]
            for k in range(j + 1, 8):
                for i in range(k, 8):
                    s[i, k] = s[i, k] - l[i, j] * l[k, j]

        def solve(block):
            out = []
            for j in range(8):
                t = spread(block[j : j + 1, :])
                for k in range(j):
                    t = t - l[j, k] * out[k]
                out.append(t * inv[j])
            return out

        def back(r):
            q = [None] * 8
            for j in reversed(range(8)):
                t = r[j]
                for i in reversed(range(j + 1, 8)):
                    t = t - l[i, j] * q[i]
                q[j] = t * inv[j]
            return q

        def pack(r):
            t = r[0]
            for j in range(1, 8):
                t = jnp.where(sub == j, r[j], t)
            return t

        def tree(p):
            return ((p[0] + p[1]) + (p[2] + p[3])) + ((p[4] + p[5]) + (p[6] + p[7]))

        ra = solve(ga)
        rv = solve(gv)
        u_ref[rows, :] = jnp.where(lane >= sub + 8 * g, pack(ra), 0.0)
        v_ref[rows, :] = pack(rv)
        if g < 15:
            qa = back(ra)
            qv = back(rv)
            for h in range(g + 1, 16):
                below = slice(8 * h, 8 * h + 8)
                a = a_ref[below, :]
                v = v_ref[below, :]
                m = [spread(a[:, 8 * g + j : 8 * g + j + 1]) for j in range(8)]
                a_ref[below, :] = a - tree([m[j] * qa[j] for j in range(8)])
                v_ref[below, :] = v - tree([m[j] * qv[j] for j in range(8)])


def step_kernel(k, *refs):
    if k == 0:
        d_ref, w_ref, outs = refs[0], None, refs[1:]
    else:
        d_ref, w_ref, outs = refs[0], refs[1], refs[2:]
    if k < 3:
        p_ref, vrow_ref, dn_ref, wn_ref, a_ref, t_ref, u_ref = outs
    else:
        p_ref, vrow_ref, a_ref, t_ref, u_ref = outs
    a_ref[...] = d_ref[0:128, 0:128]
    factor128(a_ref, t_ref, u_ref)
    t = t_ref[...]
    p_ref[0:128, :] = u_ref[...].T
    if k:
        vrow_ref[:, 0 : 128 * k] = dot(t, w_ref[0:128, :], NN)
    vrow_ref[:, 128 * k :] = t
    if k < 3:
        p_ref[128:, :] = dot(d_ref[128:, 0:128], t, TN)
        for j in range(1, 4 - k):
            dn_ref[128 * (j - 1) :, 128 * (j - 1) : 128 * j] = d_ref[128 * j :, 128 * j : 128 * j + 128] - dot(
                p_ref[128 * j :, :], p_ref[128 * j : 128 * j + 128, :], TN
            )
        if k:
            wn_ref[:, 0 : 128 * k] = w_ref[128:, :] - dot(p_ref[128:, :], vrow_ref[:, 0 : 128 * k], NN)
        wn_ref[:, 128 * k :] = -dot(p_ref[128:, :], t, NN)


def step(k, d, w):
    n = (4 - k) * 128
    f = lambda *s: jax.ShapeDtypeStruct(s, jnp.float32)
    outs = [f(n, 128), f(128, 128 * (k + 1))]
    if k < 3:
        outs += [f(n - 128, n - 128), f(n - 128, 128 * (k + 1))]
    return pl.pallas_call(
        functools.partial(step_kernel, k),
        out_shape=outs,
        name=f"panel{k}",
        scratch_shapes=[pltpu.VMEM((128, 128), jnp.float32)] * 3,
        compiler_params=pltpu.CompilerParams(vmem_limit_bytes=40 * 2**20),
        cost_estimate=pl.CostEstimate(flops=7 * 10**9, bytes_accessed=8 * n * n, transcendentals=0),
    )(*((d,) if k == 0 else (d, w)))


def whole_call(kernel, name, out_shape, scratch, flops, *args):
    vm = pl.BlockSpec(memory_space=pltpu.VMEM)
    sm = pl.BlockSpec(memory_space=pltpu.SMEM)
    return pl.pallas_call(
        kernel,
        out_shape=[jax.ShapeDtypeStruct(s, t) for s, t in out_shape],
        name=name,
        in_specs=[sm if a.dtype == jnp.int32 else vm for a in args],
        out_specs=[vm] * len(out_shape),
        scratch_shapes=[pltpu.VMEM(s, jnp.float32) for s in scratch],
        compiler_params=pltpu.CompilerParams(vmem_limit_bytes=48 * 2**20),
        cost_estimate=pl.CostEstimate(flops=flops, bytes_accessed=8 * 2**20, transcendentals=0),
    )(*args)


def factor512(d, between=lambda k, d: d):
    w, ps, vs = None, [], []
    for k in range(4):
        o = step(k, d, w)
        ps.append(o[0])
        vs.append(o[1])
        if k < 3:
            d, w = between(k, o[2]), o[3]
    return ps, vs


def unpack(pack_ref, v_s):
    v_s[...] = jnp.zeros_like(v_s)
    n = 0
    for k in range(4):
        for j in range(k + 1):
            v_s[128 * k : 128 * k + 128, 128 * j : 128 * j + 128] = pack_ref[128 * n : 128 * n + 128, :]
            n += 1


def pack(vs):
    return jnp.concatenate([vs[k][:, 128 * j : 128 * j + 128] for k in range(4) for j in range(k + 1)], axis=0)


def join_kernel(low_ref, next_ref, *refs):
    vs, pack_ref, d_ref, v_s, x_s = refs[0:4], *refs[4:8]
    v_s[...] = jnp.zeros_like(v_s)
    n = 0
    for k in range(4):
        v_s[128 * k : 128 * k + 128, 0 : 128 * (k + 1)] = vs[k][...]
        for j in range(k + 1):
            pack_ref[128 * n : 128 * n + 128, :] = vs[k][:, 128 * j : 128 * j + 128]
            n += 1
    x_s[...] = dot(low_ref[...], v_s[...], TN)
    d_ref[...] = next_ref[...] - dot(x_s[...], x_s[...], TN)
    q = dot(x_s[...], v_s[...], NN)
    for j in range(4):
        pack_ref[1280 + 512 * j : 1792 + 512 * j, :] = q[:, 128 * j : 128 * j + 128]


def unit(c, want):
    ri = lax.broadcasted_iota(jnp.int32, (512, 512), 0)
    ci = lax.broadcasted_iota(jnp.int32, (512, 512), 1)
    return jnp.where((ri == ci) & (c == want), -1.0, 0.0).astype(jnp.float32)


def early_kernel(c_ref, b_ref, pack_ref, r_ref, n_ref, b_s, v_s, q_s, y_s):
    c = c_ref[0]
    for i in range(4):
        b_s[128 * i : 128 * i + 128, :] = b_ref[(8 - i) % 8]
        q_s[:, 128 * i : 128 * i + 128] = pack_ref[1280 + 512 * i : 1792 + 512 * i, :]
    unpack(pack_ref, v_s)
    late = dot(b_s[...], q_s[...], TN)
    for i in range(4):
        r_ref[128 * i : 128 * i + 128, :] = b_ref[1 + i] - late[128 * i : 128 * i + 128, :]
    y_s[...] = dot(v_s[...], b_s[...], TN)

    @pl.when(c < 2)
    def _():
        y_s[...] = unit(c, 0)

    n_ref[...] = dot(v_s[...], y_s[...], TT)


def late_kernel(c_ref, pack0_ref, pack1_ref, r_ref, n_ref, hi_ref, lo_ref, v_s, q_s, y_s):
    c = c_ref[0]
    for i in range(4):
        q_s[:, 128 * i : 128 * i + 128] = pack0_ref[1280 + 512 * i : 1792 + 512 * i, :]
    unpack(pack1_ref, v_s)
    y_s[...] = dot(v_s[...], r_ref[...], TN)

    @pl.when(c < 2)
    def _():
        y_s[...] = unit(c, 1)

    m1 = dot(v_s[...], y_s[...], TT)
    y_s[...] = m1
    m0 = n_ref[...] - dot(q_s[...], y_s[...], TT)
    for i, m in enumerate((m0, m1)):
        hi = m.astype(jnp.bfloat16)
        hi_ref[512 * i : 512 * i + 512, :] = hi
        lo_ref[512 * i : 512 * i + 512, :] = (m - hi.astype(jnp.float32)).astype(jnp.bfloat16)


def update_kernel(place_ref, a_ref, *refs):
    hi_ref, lo_ref, f_ref, out_ref = refs[8:]
    r, c = place_ref[0], place_ref[1]
    slot = pl.program_id(0)
    lower = 8 * slot + r >= c
    diagonal = (slot == 0) & (c < 2) & (r == c)

    @pl.when(lower & jnp.logical_not(diagonal))
    def _():
        total = jnp.where(c < 2, 0.0, a_ref[0])
        for p in range(2):
            rows = jnp.concatenate([ref[0] for ref in refs[4 * p : 4 * p + 4]], axis=0)
            hi = rows.astype(jnp.bfloat16)
            lo = (rows - hi.astype(jnp.float32)).astype(jnp.bfloat16)
            mh = hi_ref[512 * p : 512 * p + 512, :]
            ml = lo_ref[512 * p : 512 * p + 512, :]
            one = lambda u, v: lax.dot_general(u, v, (NN, ((), ())), preferred_element_type=jnp.float32)
            total = total - (one(hi, mh) + (one(hi, ml) + one(lo, mh)))
        out_ref[0] = total

    @pl.when(jnp.logical_not(lower))
    def _():
        out_ref[...] = jnp.zeros_like(out_ref)

    @pl.when(diagonal)
    def _():
        out_ref[0] = f_ref[...]


def update(place, local, rows, hi, lo, factor):
    vm = pl.BlockSpec(memory_space=pltpu.VMEM)
    tile = pl.BlockSpec((1, 512, 512), lambda s: (s, 0, 0))
    part = lambda q: pl.BlockSpec((1, 128, 512), lambda s: (8 * s + q, 0, 0))
    return pl.pallas_call(
        update_kernel,
        grid=(4,),
        out_shape=jax.ShapeDtypeStruct((4, 512, 512), jnp.float32),
        name="update",
        in_specs=[pl.BlockSpec(memory_space=pltpu.SMEM), tile] + [part(q) for q in (0, 7, 6, 5, 1, 2, 3, 4)] + [vm] * 3,
        out_specs=tile,
        compiler_params=pltpu.CompilerParams(vmem_limit_bytes=60 * 2**20),
        cost_estimate=pl.CostEstimate(flops=6 * 10**9, bytes_accessed=16 * 2**20, transcendentals=0),
    )(place, local, *[rows] * 8, hi, lo, factor)


def body(matrix):
    r = lax.axis_index("row")
    c = lax.axis_index("col")
    x, y, z = c // NZ, r // 2, c % NZ
    even = lax.rem(r, 2) == 0
    local = matrix.reshape(4, 512, 512)
    R, X, Z, C = range(8), range(4), range(8), range(32)
    tie = lax.optimization_barrier
    swap = lambda v: permute(v, [(gid(a, b), gid(a ^ 1, b)) for a in R for b in C])
    from_x0 = lambda v, d: permute(v, [(gid(a, p), gid(a, 8 * d + p)) for a in R for p in (0, 1)])
    over_y = lambda v, d: permute(v, [(gid(k, 0), gid(2 * d + k, 0)) for k in (0, 1)])
    over_z = lambda v, d: permute(v, [(gid(a, 0), gid(a, d)) for a in R])
    over_x = lambda v, d: permute(v, [(gid(a, b), gid(a, 8 * d + b)) for a in R for b in Z])
    shift_y = lambda v, d: permute(v, [(gid(a, b), gid((a + 2 * d) % 8, b)) for a in R for b in C])

    def stage_y(parts):
        return [jnp.where(y == 0, parts[0], 0.0)] + [over_y(parts[d], d) for d in (2, 1, 3)]

    def stage_z(got):
        return [jnp.where(z == 0, got, 0.0)] + [over_z(got, d) for d in (4, 3, 5, 2, 6, 1, 7)]

    def stage_x(got):
        return [jnp.where(x == 0, got, 0.0)] + [over_x(got, d) for d in (2, 1, 3)]

    def stage_ring(got):
        return [got] + [shift_y(got, d) for d in (1, 2, 3)]

    def gather_ring(parts):
        whole = jnp.zeros((4,) + parts[0].shape, jnp.float32)
        for d in range(4):
            whole = lax.dynamic_update_index_in_dim(whole, parts[d], lax.rem(y + 4 - d, 4), 0)
        return whole

    halves = lambda v: jnp.where(even, v[: v.shape[0] // 2], v[v.shape[0] // 2 :])
    quarters = lambda v: v.reshape(4, v.shape[0] // 4, 128)

    slots = [from_x0(local[1], 1), from_x0(local[3], 3), from_x0(local[2], 2)]
    piece, below, corner = [], None, None

    def between(k, d):
        nonlocal below, corner
        if k == 0:
            held, d = tie((local, d))
            below = swap(held[0])
            corner = permute(held[0], [(gid(1, 1), gid(0, 0))])
        return d

    f32, b16 = jnp.float32, jnp.bfloat16
    tile, sq = (512, 512), ((512, 512), jnp.float32)
    me = c.reshape(1)
    full = lambda q: jnp.concatenate([jnp.pad(q[k], ((128 * k, 0), (0, 0))) for k in range(4)], axis=1)
    ps0, vs0 = factor512(local[0], between)
    pack0, corner = whole_call(join_kernel, "join", [((3328, 128), f32), sq], [tile, tile], 5 * 10**9, below, corner, *vs0)
    one = swap(pack0[1664:])
    rows, mine = None, None

    def beside(k, d):
        nonlocal one, slots, piece, rows, mine
        if k == 0:
            one, slots, d = tie((one, slots, d))
            one = stage_y(quarters(jnp.where(even, pack0[:1664], one)))
            slot = jnp.where(x == 0, local[0], sum(slots))
            piece.append(jnp.where(z < 2, slot[0:128], 0.0))
            for e in (1, 2, 3):
                pairs = [(gid(a, 8 * b + p), gid(a, 8 * b + (1 + e if p else 8 - e))) for a in R for b in X for p in (0, 1)]
                piece.append(permute(slot[128 * e : 128 * e + 128], pairs))
        elif k == 1:
            one, d = tie((one, d))
            one = stage_z(sum(one))
        else:
            piece, d = tie((piece, d))
            piece = sum(piece)
            rows = lax.all_gather(piece, "col", tiled=True).reshape(32, 128, 512)
            mine = permute(piece, [(gid(a, 8 * b + e), gid(e, 8 * b + a)) for a in R for b in X for e in Z])
        return d

    def both(mine):
        other = swap(mine)
        return jnp.concatenate([jnp.where(even, mine, other), jnp.where(even, other, mine)], axis=0)

    ps1, vs1 = factor512(corner, beside)
    pack1 = pack(vs1)
    two, one = tie((swap(pack1[640:]), one))
    one = stage_x(sum(one))
    two = stage_y(quarters(jnp.where(even, pack1[:640], two)))
    one, two, ps1, mine = tie((one, two, ps1, mine))
    one, two, quad = stage_ring(sum(one)), stage_z(sum(two)), stage_ring(mine)
    factor1 = permute(full(ps1), [(gid(0, 0), gid(1, 1))])
    factor = jnp.where(c == 0, full(ps0), factor1)
    one, two, quad = tie((one, two, quad))
    pack0 = both(gather_ring(one).reshape(1664, 128))
    quad.append(swap(jnp.stack(quad)))
    two = stage_x(sum(two))
    two, quad, pack0 = tie((two, quad, pack0))
    two = stage_ring(sum(two))
    mate = r + 1 - 2 * lax.rem(r, 2)
    b_col = jnp.zeros((8, 128, 512), jnp.float32)
    for d in range(4):
        b_col = lax.dynamic_update_index_in_dim(b_col, quad[d], lax.rem(r + 8 - 2 * d, 8), 0)
        b_col = lax.dynamic_update_index_in_dim(b_col, quad[4][d], lax.rem(mate + 8 - 2 * d, 8), 0)
    rest, first = whole_call(early_kernel, "early", [sq, sq], [tile] * 4, 6 * 10**9, me, b_col, pack0)
    two, rest = tie((two, rest))
    pack1 = both(gather_ring(two).reshape(640, 128))
    hi, lo = whole_call(late_kernel, "late", [((1024, 512), b16)] * 2, [tile] * 3, 6 * 10**9, me, pack0, pack1, rest, first)
    out = update(jnp.stack([r, c]), local, rows, hi, lo, factor)
    return out.reshape(4, 1, 1, 1, 512, 512)


def solution(mesh):
    placed = P(None, "row", None, "col", None, None)
    return jax.shard_map(body, mesh=mesh, in_specs=(placed,), out_specs=placed, check_vma=False)
```
